1024 devices in a mesh: exp: 16 (over x, z_hi), dp: 64 (over y, z_lo, core).
Axes of the slice: x: 4, y: 8, z: 16 (z_hi: 4, z_lo: 4; z = z_hi * 4 + z_lo), core: 2. Of those that a mesh axis runs over, the one named last changes fastest.
Arguments:
- tokens: bfloat16 [8192, 3584], P('dp', 'exp'), may hold values from -6 to 6
- cotangent: bfloat16 [8192, 3584], P('dp', 'exp'), may hold values from -6 to 6
- expert_ids: int32 [8192, 1], P('dp'), may hold values from 0 to 63; in each aligned block of 128 rows (0 to 127, 128 to 255, ...) at most 4 rows name the same one
- gate_prob: bfloat16 [8192], P('dp'), may hold values from 0.099609375 to 1
- w_gate: bfloat16 [64, 1024, 3584], P('dp', 'exp'), may hold values from -0.09375 to 0.09375
- w_up: bfloat16 [64, 1024, 3584], P('dp', 'exp'), may hold values from -0.09375 to 0.09375
- w_down: bfloat16 [64, 1024, 3584], P('dp', 'exp'), may hold values from -0.1875 to 0.1875
Outputs:
- token_grad: bfloat16 [8192, 3584], P('dp', 'exp')
- prob_grad: float32 [8192], P('dp')
- gate_grad: bfloat16 [64, 1024, 3584], P('dp', 'exp')
- up_grad: bfloat16 [64, 1024, 3584], P('dp', 'exp')
- down_grad: bfloat16 [64, 1024, 3584], P('dp', 'exp')
The draws below stay inside these ranges and needn't reach their ends.
Inputs may be any that keep to these rules, and one draw needn't show every extreme that they name: `expert_ids`: among the 128 rows of one data shard no expert is named more than 4 times, a bound that some block reaches.
All inputs are finite; a program needn't handle non-finite values.
Results may differ from the reference program's by a relative error of at most 0.005.
Values may be sent and summed in bfloat16 or wider, within the bound.
A program may use at most 32 MiB of HBM per device.

```python
import math
import jax
import jax.numpy as jnp
import numpy as np
from jax import lax

D = 3584
FF = 1024
TOK_DEV = 128
EXPERTS = 64
CAP = 4
TOKENS = 8192
N_DP = 64


def block_levels(own_key, shape, pieces, low, high):
    level = 1.0
    for dim, blocks in pieces:
        steps = jax.random.uniform(jax.random.fold_in(jax.random.fold_in(own_key, 6), dim), (blocks,), jnp.float32, low / len(pieces), high / len(pieces))
        level = level * jnp.repeat(jnp.exp(steps), shape[dim] // blocks).reshape((-1,) + (1,) * (len(shape) - 1 - dim))
    return level


def deal_out(stream_key, own, number, rows, count, top, most, lean):
    sequence = jax.random.permutation(stream_key, count)
    heavy_load, common = portions_of(count, rows * top, most, lean, True), portions_of(count, rows * top, most, lean, False)
    places = jnp.arange(count)

    def named(lengths, turn):
        used = int((lengths > 0).sum())
        fixed = max(1, used // 4)
        passed = fixed + (places - fixed + turn * (used - fixed)) % max(1, count - fixed)
        return jnp.zeros((count,), jnp.int32).at[sequence[jnp.where(places < fixed, places, passed)]].set(jnp.asarray(lengths, jnp.int32))

    lengths = jnp.where(number % 4 == 0, named(heavy_load, number // 4), named(common, number - number // 4 - 1))
    mixed = jax.random.permutation(jax.random.fold_in(own, 3), count)
    donor, taker = mixed[0:count // 2 * 2:2], mixed[1:count // 2 * 2:2]
    room = jnp.minimum(lengths[donor] - 1, most - lengths[taker]) // 2
    room = jnp.where((donor == sequence[0]) | (taker == sequence[0]) | (lengths[taker] == 0), 0, jnp.maximum(room, 0))
    passed = jax.random.randint(jax.random.fold_in(own, 4), (count // 2,), 0, 1 << 20) % (room + 1)
    lengths = lengths.at[donor].add(-passed).at[taker].add(passed)
    members = jnp.searchsorted(jnp.cumsum(lengths), jnp.arange(rows * top), side="right").astype(jnp.int32)
    grid = members.reshape(top, rows).T
    grid = grid[jax.random.permutation(jax.random.fold_in(own, 1), rows)]
    turn = jax.random.randint(jax.random.fold_in(own, 2), (rows, 1), 0, top)
    return jnp.take_along_axis(grid, (jnp.arange(top)[None, :] + turn) % top, axis=1)


def portions_of(number_of, total, most, slope, full):
    portions = [(1 << 20) // math.isqrt(grade ** slope) + 1 for grade in range(1, number_of + 1)]
    largest = most if full else min(most, max(-(-total // number_of), total * portions[0] // sum(portions)))
    least = 1 if total - largest >= number_of - 1 else 0
    counts, spare = [largest] + [least] * (number_of - 1), total - largest - least * (number_of - 1)
    while spare > 0:
        candidates = [i for i in range(1, number_of) if counts[i] < largest] or [i for i in range(1, number_of) if counts[i] < most]
        pool, left = sum([portions[i] for i in candidates]), spare
        for i in candidates:
            more = min(most - counts[i], max(1, left * portions[i] // pool), spare)
            counts[i] = counts[i] + more
            spare = spare - more
    return np.array(counts)


def centred(rng, extent, width, bound, pieces=(), held_as=jnp.bfloat16):
    array = jax.random.normal(rng, extent, jnp.float32) * width
    if len(pieces) > 0:
        array = block_levels(rng, extent, pieces, -0.22, 0.18) * array
    return jnp.clip(array, min=-bound, max=bound).astype(held_as)


def setup_inputs(seed: int = 0) -> dict:
    arg_keys = jax.random.split(jax.random.key(seed), 8)
    tokens = centred(arg_keys[0], (TOKENS, D), 1.0, 6.0, ((0, 64), (1, 16)))
    cotangent = centred(arg_keys[1], (TOKENS, D), 1.0, 6.0, ((0, 64), (1, 16)))
    expert_ids_keys = jax.random.split(jax.random.fold_in(arg_keys[2], 1), TOKENS // TOK_DEV)
    expert_ids_turns = jax.random.permutation(jax.random.fold_in(arg_keys[2], 3), TOKENS // TOK_DEV)
    expert_ids = jax.vmap(lambda own, number: deal_out(jax.random.fold_in(arg_keys[2], 2), own, number, TOK_DEV, EXPERTS, 1, CAP, 2))(expert_ids_keys, expert_ids_turns).reshape((TOKENS, 1))
    gate_prob = jnp.clip(jnp.exp(math.log(1.0) - 2.306499 * jax.random.uniform(arg_keys[3], (TOKENS,), jnp.float32) ** block_levels(arg_keys[3], (TOKENS,), ((0, 64),), -0.2, 0.2)), 0.099609375, 1.0).astype(jnp.bfloat16)
    w_gate = centred(arg_keys[4], (EXPERTS, FF, D), D ** -0.5, 0.09375, ((0, 64), (1, 16)))
    w_up = centred(arg_keys[5], (EXPERTS, FF, D), D ** -0.5, 0.09375, ((0, 64), (1, 16)))
    w_down = centred(arg_keys[6], (EXPERTS, FF, D), FF ** -0.5, 0.1875, ((0, 64), (1, 16)))
    return dict(tokens=tokens, cotangent=cotangent, expert_ids=expert_ids, gate_prob=gate_prob, w_gate=w_gate, w_up=w_up, w_down=w_down)


def expert_pass(tokens_padded, cotangent_padded, prob_padded, table, gate_panel, up_panel, down_panel):
    rows_in = tokens_padded[table]
    rows_back = cotangent_padded[table]
    weight_rows = prob_padded[table].astype(jnp.float32)[:, None]
    gate = jnp.dot(rows_in, gate_panel.T, preferred_element_type=jnp.float32)
    upper = jnp.dot(rows_in, up_panel.T, preferred_element_type=jnp.float32)
    sigmoid_gate = jax.nn.sigmoid(gate)
    hidden = gate * sigmoid_gate * upper
    back = jnp.dot(rows_back, down_panel.T, preferred_element_type=jnp.float32)
    prob_part = jnp.sum(hidden * back, axis=1)
    hidden_grad = weight_rows * back
    up_delta = (hidden_grad * gate * sigmoid_gate).astype(jnp.bfloat16)
    gate_delta = (hidden_grad * upper * sigmoid_gate * (1.0 + gate * (1.0 - sigmoid_gate))).astype(jnp.bfloat16)
    scaled = (weight_rows * hidden).astype(jnp.bfloat16)
    down_grad = jnp.dot(scaled.T, rows_back, preferred_element_type=jnp.float32).astype(jnp.bfloat16)
    gate_grad = jnp.dot(gate_delta.T, rows_in, preferred_element_type=jnp.float32).astype(jnp.bfloat16)
    up_grad = jnp.dot(up_delta.T, rows_in, preferred_element_type=jnp.float32).astype(jnp.bfloat16)
    token_rows = jnp.dot(gate_delta, gate_panel, preferred_element_type=jnp.float32) + jnp.dot(up_delta, up_panel, preferred_element_type=jnp.float32)
    return gate_grad, up_grad, down_grad, token_rows, prob_part


def reference(tokens, cotangent, expert_ids, gate_prob, w_gate, w_up, w_down):
    chosen = expert_ids[:, 0].astype(jnp.int32)
    onehot = (chosen[:, None] == jnp.arange(EXPERTS, dtype=jnp.int32)[None, :]).astype(jnp.int32)
    blocks = onehot.reshape(N_DP, TOK_DEV, EXPERTS)
    earlier = jnp.cumsum(blocks, axis=1) - blocks
    slot_index = jnp.sum(earlier * blocks, axis=2).reshape(TOKENS).astype(jnp.int32)
    source = (jnp.arange(TOKENS, dtype=jnp.int32) // TOK_DEV).astype(jnp.int32)
    position = (chosen * (N_DP * CAP) + source * CAP + slot_index).astype(jnp.int32)
    table = jnp.full((EXPERTS * N_DP * CAP,), TOKENS, dtype=jnp.int32)
    table = table.at[position].set(jnp.arange(TOKENS, dtype=jnp.int32)).reshape(EXPERTS, N_DP * CAP)
    tokens_padded = jnp.concatenate([tokens, jnp.zeros((1, D), tokens.dtype)], axis=0)
    cotangent_padded = jnp.concatenate([cotangent, jnp.zeros((1, D), cotangent.dtype)], axis=0)
    prob_padded = jnp.concatenate([gate_prob, jnp.zeros((1,), gate_prob.dtype)], axis=0)

    def one_expert(items):
        return expert_pass(tokens_padded, cotangent_padded, prob_padded, items[0], items[1], items[2], items[3])

    gate_grad, up_grad, down_grad, token_rows, prob_part = lax.map(one_expert, (table, w_gate, w_up, w_down))
    token_grad = token_rows.reshape(EXPERTS * N_DP * CAP, D)[position].astype(jnp.bfloat16)
    prob_grad = prob_part.reshape(EXPERTS * N_DP * CAP)[position]
    return token_grad, prob_grad, gate_grad, up_grad, down_grad
```

```python
import functools

import jax
import jax.numpy as jnp
from jax import lax
from jax.experimental import pallas as pl
from jax.experimental.pallas import tpu as pltpu
from jax.sharding import PartitionSpec as P

MESH = pl.DeviceIdType.MESH
BF = jnp.bfloat16
F32 = jnp.float32
NT = (((1,), (1,)), ((), ()))
NN = (((1,), (0,)), ((), ()))
TN = (((0,), (0,)), ((), ()))


def iota(shape, dim):
    return lax.broadcasted_iota(jnp.int32, shape, dim)


def dot(a, b, dims):
    return lax.dot_general(a, b, dims, preferred_element_type=F32)


def pack(left, right):
    lane = iota((192, 128), 1)
    tail = right[192:256]
    moved = jnp.concatenate([pltpu.roll(tail, 96, 1), pltpu.roll(tail, 64, 1), pltpu.roll(tail, 32, 1)], axis=0)
    return jnp.concatenate([left, jnp.where(lane < 96, right[0:192], moved)], axis=0)


def unpack(packed):
    lane = iota((192, 128), 1)
    low = iota((64, 128), 1)
    rest = packed[256:448]
    top = jnp.where(lane < 96, rest, 0.0)
    tail = jnp.where(
        low < 32,
        pltpu.roll(rest[0:64], 32, 1),
        jnp.where(
            low < 64,
            pltpu.roll(rest[64:128], 64, 1),
            jnp.where(low < 96, pltpu.roll(rest[128:192], 96, 1), 0.0),
        ),
    )
    return packed[0:256], jnp.concatenate([top, tail], axis=0)


def shift_left(a, b, count):
    lane = iota(a.shape, 1)
    return jnp.where(lane < 128 - count, pltpu.roll(a, 128 - count, 1), pltpu.roll(b, 128 - count, 1))


def kernel(
    n_dp,
    ids_ref, prob_ref, tok_ref, cot_ref, wg_ref, wu_ref, wd_ref,
    tg_ref, pg_ref, gg_ref, ug_ref, dg_ref,
    sbuf, rbuf, zbuf, wbuf, wpad, tpad, full, gusend, gurecv, bsend, brecv, scal, delt,
    pbx, pbz, pxr, pzr, rs1s, rs1r, rs2s, rs2r, rets, retr, gradb, ssem, rsem, lsem,
):
    exp = lax.axis_index("exp")
    me = lax.axis_index("dp")
    x, z = exp // 4, exp % 4
    xs = [(x + k) % 4 for k in range(4)]
    zs = [(z + k) % 4 for k in range(4)]

    def x_dev(k):
        return {"exp": xs[k] * 4 + z, "dp": me}

    def z_dev(k):
        return {"exp": x * 4 + zs[k], "dp": me}

    counter = [0]

    def remote(src, dst, dev):
        i = counter[0]
        counter[0] += 1
        return pltpu.make_async_remote_copy(
            src_ref=src, dst_ref=dst, send_sem=ssem.at[i], recv_sem=rsem.at[i],
            device_id=dev, device_id_type=MESH,
        )

    pending = []

    def start(copy):
        copy.start()
        pending.append(copy)
        return copy

    barrier = pltpu.get_barrier_semaphore()

    def greet(k, carry):
        pl.semaphore_signal(barrier, inc=1, device_id={"exp": exp, "dp": (me + k) % n_dp}, device_id_type=MESH)
        return carry

    lax.fori_loop(1, n_dp, greet, 0)
    for k in range(1, 4):
        pl.semaphore_signal(barrier, inc=1, device_id=x_dev(k), device_id_type=MESH)
        pl.semaphore_signal(barrier, inc=1, device_id=z_dev(k), device_id_type=MESH)

    own_w = []
    for a, ref in enumerate((wg_ref, wu_ref, wd_ref)):
        copy = pltpu.make_async_copy(
            ref.at[:, pl.ds(pl.multiple_of(x * 896, 128), 896)], wbuf.at[a, x], lsem.at[a]
        )
        copy.start()
        own_w.append(copy)

    ids = ids_ref[...]
    hot = (iota((n_dp, 128), 0) == ids).astype(F32)
    before = (iota((128, 128), 0) < iota((128, 128), 1)).astype(BF)
    earlier = dot(hot.astype(BF), before, NN)
    slot = jnp.sum(hot * earlier, axis=0, keepdims=True)
    position = ids.astype(F32) * 4.0 + slot

    rows = iota((16 * n_dp, 128), 0)
    row_slot = ((rows >> 4) * 4 + (rows & 3)).astype(F32)
    row_part = (rows >> 2) & 3
    placing = jnp.where(row_slot == position, 1.0, 0.0).astype(BF)
    prob_block = jnp.where(iota((32, 128), 0) == 0, prob_ref[...].astype(F32), 0.0).astype(BF)
    out = dot(placing, tok_ref[0:128], NT)
    out = jnp.where(row_part == 1, dot(placing, jnp.concatenate([tok_ref[128:224], prob_block], axis=0), NT), out)
    out = jnp.where(row_part == 2, dot(placing, cot_ref[0:128], NT), out)
    zero_block = jnp.zeros((32, 128), BF)
    out = jnp.where(row_part == 3, dot(placing, jnp.concatenate([cot_ref[128:224], zero_block], axis=0), NT), out)
    sbuf[...] = out.astype(BF).reshape(n_dp, 16, 128)

    pl.semaphore_wait(barrier, n_dp - 1 + 6)

    i_disp = counter[0]
    counter[0] += 1

    def send(k, carry):
        to = (me + k) % n_dp
        pltpu.make_async_remote_copy(
            src_ref=sbuf.at[to], dst_ref=rbuf.at[me], send_sem=ssem.at[i_disp], recv_sem=rsem.at[i_disp],
            device_id={"exp": exp, "dp": to}, device_id_type=MESH,
        ).start()
        return carry

    lax.fori_loop(1, n_dp, send, 0)
    rbuf[me] = sbuf[me]

    w_copies = [
        [
            start(remote(
                ref.at[:, pl.ds(pl.multiple_of(xs[k] * 896, 128), 896)], wbuf.at[a, x], x_dev(k)
            ))
            for k in range(1, 4)
        ]
        for a, ref in enumerate((wg_ref, wu_ref, wd_ref))
    ]

    dispatched = pltpu.make_async_remote_copy(
        src_ref=sbuf.at[pl.ds(0, n_dp - 1)], dst_ref=rbuf.at[pl.ds(0, n_dp - 1)],
        send_sem=ssem.at[i_disp], recv_sem=rsem.at[i_disp], device_id={"exp": exp, "dp": me}, device_id_type=MESH,
    )
    dispatched.wait_recv()

    o, i = iota((256, 256), 0), iota((256, 256), 1)
    order = jnp.where(i == ((o >> 2) & 15) * 16 + (o >> 6) * 4 + (o & 3), 1.0, 0.0).astype(BF)
    groups = []
    for g in range(n_dp // 16):
        groups.append(dot(order, rbuf[16 * g:16 * g + 16].reshape(256, 128), NN))
    parts = [jnp.concatenate([group[64 * j:64 * j + 64] for group in groups], axis=0) for j in range(4)]
    pick = jnp.where((iota((8, 128), 0) == 0) & (iota((8, 128), 1) == 96), 1.0, 0.0).astype(BF)
    weight = dot(pick, parts[1].astype(BF), NT)[0:1]

    def gather_start(a):
        mine = zbuf.at[a, z]
        halves = [mine.at[pl.ds(0, 224)], mine.at[pl.ds(224, 224)]]
        right = [remote(halves[0], halves[0], z_dev(1)), remote(halves[1], halves[1], z_dev(1))]
        left = [remote(halves[1], halves[1], z_dev(3)), remote(halves[0], halves[0], z_dev(3))]
        for n in range(2):
            start(right[n])
            start(left[n])
        return right, left

    def gather_forward(a, right, left):
        from_left = zbuf.at[a, zs[3], pl.ds(0, 224)]
        from_right = zbuf.at[a, zs[1], pl.ds(224, 224)]
        onward_right = remote(from_left, from_left, z_dev(1))
        onward_left = remote(from_right, from_right, z_dev(3))
        right[0].wait_recv()
        start(onward_right)
        left[0].wait_recv()
        start(onward_left)
        return [right[1], left[1], onward_right, onward_left]

    zbuf[0, z] = pack(parts[0], parts[1]).astype(BF)
    t_right, t_left = gather_start(0)
    zbuf[1, z] = pack(parts[2], parts[3]).astype(BF)
    t_rest = gather_forward(0, t_right, t_left)
    for copy in t_right + t_left:
        copy.wait_send()
    pending[:] = [copy for copy in pending if not any(copy is done for done in t_right + t_left)]
    c_right, c_left = gather_start(1)

    def shift_weights(a):
        own_w[a].wait()
        for copy in w_copies[a]:
            copy.wait_recv()
        whole = wbuf[a].reshape(256, 896)
        block = [whole[:, 128 * b:128 * b + 128].astype(F32) for b in range(7)]
        wpad[a, 0] = whole[:, 0:256]
        for n, (first, count) in enumerate(((1, 96), (3, 64), (5, 32))):
            wpad[a, n + 1, :, 0:128] = shift_left(block[first], block[first + 1], count).astype(BF)
            last = block[first + 2] if first + 2 < 7 else block[first + 1]
            wpad[a, n + 1, :, 128:256] = shift_left(block[first + 1], last, count).astype(BF)

    def unpack_all(a):
        for n in range(4):
            left, right = unpack(zbuf[a, n].astype(F32))
            tpad[a, n, :, 0:128] = left.astype(BF)
            tpad[a, n, :, 128:256] = right.astype(BF)

    def join_all(a):
        part = [[tpad[a, n, :, 128 * h:128 * h + 128].astype(F32) for h in range(2)] for n in range(4)]
        nothing = jnp.zeros((256, 128), F32)
        block = [nothing] * 7
        block[0], block[1] = part[0]
        for n, (first, count) in enumerate(((1, 96), (3, 64), (5, 32))):
            lo, hi = part[n + 1]
            block[first] += shift_left(nothing, lo, 128 - count)
            block[first + 1] += shift_left(lo, hi, 128 - count)
            if first + 2 < 7:
                block[first + 2] += shift_left(hi, nothing, 128 - count)
        for b in range(7):
            full[a, :, 128 * b:128 * b + 128] = block[b].astype(BF)

    def project(a, t):
        total = dot(wpad[a, 0], tpad[t, 0], NT)
        for n in range(1, 4):
            total += dot(wpad[a, n], tpad[t, n], NT)
        return total.reshape(4, 64, 256)

    shift_weights(0)
    shift_weights(1)
    for copy in t_rest:
        copy.wait_recv()
    unpack_all(0)
    gusend[:, 0] = project(0, 0)
    gusend[:, 1] = project(1, 0)
    gu_copies = [start(remote(gusend.at[xs[k]], gurecv.at[k - 1], x_dev(k))) for k in range(1, 4)]
    shift_weights(2)
    c_rest = gather_forward(1, c_right, c_left)
    for copy in gu_copies:
        copy.wait_recv()
    gate = gusend[x, 0] + gurecv[0, 0] + gurecv[1, 0] + gurecv[2, 0]
    upper = gusend[x, 1] + gurecv[0, 1] + gurecv[1, 1] + gurecv[2, 1]
    sigmoid = jax.nn.sigmoid(gate)
    hidden = gate * sigmoid * upper
    scal[x] = (weight * hidden).astype(BF)
    s_copies = [start(remote(scal.at[x], scal.at[x], x_dev(k))) for k in range(1, 4)]
    join_all(0)

    for copy in c_rest:
        copy.wait_recv()
    unpack_all(1)
    bsend[...] = project(2, 1)
    b_copies = [start(remote(bsend.at[xs[k]], brecv.at[k - 1], x_dev(k))) for k in range(1, 4)]
    join_all(1)

    def grad_send(a, lhs, t, ref):
        gradb[a] = dot(lhs.reshape(256, 256), full[t], NN).astype(BF).reshape(4, 64, 896)
        return [
            start(remote(gradb.at[a, xs[k]], ref.at[:, pl.ds(pl.multiple_of(x * 896, 128), 896)], x_dev(k)))
            for k in range(1, 4)
        ]

    for copy in b_copies:
        copy.wait_recv()
    back = bsend[x] + brecv[0] + brecv[1] + brecv[2]
    grad = weight * back
    delt[0, x] = (grad * upper * sigmoid * (1.0 + gate * (1.0 - sigmoid))).astype(BF)
    delt[1, x] = (grad * gate * sigmoid).astype(BF)
    d_copies = [start(remote(delt.at[:, x], delt.at[:, x], x_dev(k))) for k in range(1, 4)]
    pbx[...] = jnp.broadcast_to(jnp.sum(hidden * back, axis=0, keepdims=True), (8, 256))
    px_copies = [start(remote(pbx, pxr.at[k - 1], x_dev(k))) for k in range(1, 4)]

    for copy in s_copies:
        copy.wait_recv()
    g_copies = grad_send(2, scal[...], 1, dg_ref)

    for copy in d_copies:
        copy.wait_recv()
    gate_delta = delt[0].reshape(256, 256)
    up_delta = delt[1].reshape(256, 256)

    def token_part(n):
        total = dot(gate_delta, wpad[0, n], TN) + dot(up_delta, wpad[1, n], TN)
        return pack(total[:, 0:128], total[:, 128:256])

    far = token_part(zs[2]).astype(BF)
    rs1s[...] = far.reshape(2, 224, 128)
    r1 = [start(remote(rs1s.at[0], rs1r.at[0], z_dev(1))), start(remote(rs1s.at[1], rs1r.at[1], z_dev(3)))]
    to_right = token_part(zs[1])
    rs2s[0, 1] = to_right[224:448].astype(BF)
    r2 = [start(remote(rs2s.at[0, 1], rs2r.at[0, 1], z_dev(1)))]
    to_left = token_part(zs[3])
    rs2s[1, 0] = to_left[0:224].astype(BF)
    r2.append(start(remote(rs2s.at[1, 0], rs2r.at[1, 0], z_dev(3))))
    for copy in px_copies:
        copy.wait_recv()
    pbz[...] = pbx[...] + pxr[0] + pxr[1] + pxr[2]
    pz_copies = [start(remote(pbz, pzr.at[k - 1], z_dev(k))) for k in range(1, 4)]
    r1[0].wait_recv()
    rs2s[0, 0] = (to_right[0:224] + rs1r[0].astype(F32)).astype(BF)
    r2.append(start(remote(rs2s.at[0, 0], rs2r.at[0, 0], z_dev(1))))
    r1[1].wait_recv()
    rs2s[1, 1] = (to_left[224:448] + rs1r[1].astype(F32)).astype(BF)
    r2.append(start(remote(rs2s.at[1, 1], rs2r.at[1, 1], z_dev(3))))

    g_copies += grad_send(0, delt[0], 0, gg_ref)
    g_copies += grad_send(1, delt[1], 0, ug_ref)
    here = token_part(z)
    for copy in pz_copies:
        copy.wait_recv()
    prob_total = (pbz[...] + pzr[0] + pzr[1] + pzr[2])[0:1]
    first = prob_total.astype(BF).astype(F32)
    second = (prob_total - first).astype(BF).astype(F32)
    third = prob_total - first - second
    eight = iota((8, 256), 0)
    terms = jnp.where(eight == 0, first, jnp.where(eight == 1, second, jnp.where(eight == 2, third, 0.0))).astype(BF)
    into = jnp.where(
        (iota((8, 128), 0) < 3) & (iota((8, 128), 1) == iota((8, 128), 0) + 96), 1.0, 0.0
    ).astype(BF)
    prob_lanes = dot(terms, into, TN)
    o, i = iota((128, 128), 0), iota((128, 128), 1)
    back_order = jnp.where(i == ((o >> 2) & 1) * 64 + (o >> 3) * 4 + (o & 3), 1.0, 0.0).astype(BF)

    for copy in r2:
        copy.wait_recv()
    both = rs2r[0].astype(F32) + rs2r[1].astype(F32)
    left, right = unpack(here + both.reshape(448, 128))
    left = left.astype(BF)
    right = (right + prob_lanes).astype(BF)
    for g in range(n_dp // 16):
        piece = jnp.concatenate([left[64 * g:64 * g + 64], right[64 * g:64 * g + 64]], axis=0)
        rets[16 * g:16 * g + 16] = dot(back_order, piece, NN).reshape(16, 8, 128)

    i_ret = counter[0]
    counter[0] += 1

    def send_back(k, carry):
        to = (me + k) % n_dp
        pltpu.make_async_remote_copy(
            src_ref=rets.at[to], dst_ref=retr.at[me], send_sem=ssem.at[i_ret], recv_sem=rsem.at[i_ret],
            device_id={"exp": exp, "dp": to}, device_id_type=MESH,
        ).start()
        return carry

    lax.fori_loop(1, n_dp, send_back, 0)
    retr[me] = rets[me]
    for a, ref in ((2, dg_ref), (0, gg_ref), (1, ug_ref)):
        ref[:, pl.ds(pl.multiple_of(x * 896, 128), 896)] = gradb[a, x]
    rows = iota((8 * n_dp, 128), 0)
    match = ((rows >> 3) * 4 + (rows & 3)).astype(F32) == position
    part = (rows >> 2) & 1
    returned = pltpu.make_async_remote_copy(
        src_ref=rets.at[pl.ds(0, n_dp - 1)], dst_ref=retr.at[pl.ds(0, n_dp - 1)],
        send_sem=ssem.at[i_ret], recv_sem=rsem.at[i_ret], device_id={"exp": exp, "dp": me}, device_id_type=MESH,
    )
    returned.wait_recv()
    arrived = retr[...].reshape(8 * n_dp, 128)
    small = arrived.astype(BF)
    tg_ref[0:128] = dot(small, jnp.where(match & (part == 0), 1.0, 0.0).astype(BF), TN).astype(BF)
    tg_ref[128:224] = dot(small, jnp.where(match & (part == 1), 1.0, 0.0).astype(BF), TN)[0:96].astype(BF)
    column = arrived[:, 96:97] + arrived[:, 97:98] + arrived[:, 98:99]
    pg_ref[...] = jnp.sum(jnp.where(match & (part == 1), column, 0.0), axis=0, keepdims=True)

    for copy in g_copies:
        copy.wait_recv()
    dispatched.wait_send()
    returned.wait_send()
    for copy in pending:
        copy.wait_send()


def shards(tokens, cotangent, expert_ids, gate_prob, w_gate, w_up, w_down):
    n_dp = lax.axis_size("dp")
    vmem = pl.BlockSpec(memory_space=pltpu.VMEM)
    hbm = pl.BlockSpec(memory_space=pl.ANY)
    grad = jax.ShapeDtypeStruct((64, 3584), BF)
    token_grad, prob_grad, gate_grad, up_grad, down_grad = pl.pallas_call(
        functools.partial(kernel, n_dp),
        out_shape=(
            jax.ShapeDtypeStruct((224, 128), BF),
            jax.ShapeDtypeStruct((1, 128), F32),
            grad, grad, grad,
        ),
        in_specs=[vmem] * 4 + [hbm] * 3,
        out_specs=[vmem] * 5,
        scratch_shapes=[
            pltpu.VMEM((n_dp, 16, 128), BF),
            pltpu.VMEM((n_dp, 16, 128), BF),
            pltpu.VMEM((2, 4, 448, 128), BF),
            pltpu.VMEM((3, 4, 64, 896), BF),
            pltpu.VMEM((3, 4, 256, 256), BF),
            pltpu.VMEM((2, 4, 256, 256), BF),
            pltpu.VMEM((2, 256, 896), BF),
            pltpu.VMEM((4, 2, 64, 256), F32),
            pltpu.VMEM((3, 2, 64, 256), F32),
            pltpu.VMEM((4, 64, 256), F32),
            pltpu.VMEM((3, 64, 256), F32),
            pltpu.VMEM((4, 64, 256), BF),
            pltpu.VMEM((2, 4, 64, 256), BF),
            pltpu.VMEM((8, 256), F32),
            pltpu.VMEM((8, 256), F32),
            pltpu.VMEM((3, 8, 256), F32),
            pltpu.VMEM((3, 8, 256), F32),
            pltpu.VMEM((2, 224, 128), BF),
            pltpu.VMEM((2, 224, 128), BF),
            pltpu.VMEM((2, 2, 224, 128), BF),
            pltpu.VMEM((2, 2, 224, 128), BF),
            pltpu.VMEM((n_dp, 8, 128), F32),
            pltpu.VMEM((n_dp, 8, 128), F32),
            pltpu.VMEM((3, 4, 64, 896), BF),
            pltpu.SemaphoreType.DMA((64,)),
            pltpu.SemaphoreType.DMA((64,)),
            pltpu.SemaphoreType.DMA((3,)),
        ],
        compiler_params=pltpu.CompilerParams(
            collective_id=0, has_side_effects=True, vmem_limit_bytes=48 * 1024 * 1024
        ),
    )(
        expert_ids.reshape(1, -1), gate_prob.reshape(1, -1), tokens.T, cotangent.T, w_gate[0], w_up[0], w_down[0]
    )
    return token_grad.T, prob_grad.reshape(-1), gate_grad[None], up_grad[None], down_grad[None]


def solution(mesh):
    in_specs = (
        P("dp", "exp"),
        P("dp", "exp"),
        P("dp", None),
        P("dp"),
        P("dp", "exp", None),
        P("dp", "exp", None),
        P("dp", "exp", None),
    )
    out_specs = (
        P("dp", "exp"),
        P("dp"),
        P("dp", "exp", None),
        P("dp", "exp", None),
        P("dp", "exp", None),
    )
    return jax.shard_map(shards, mesh=mesh, in_specs=in_specs, out_specs=out_specs, check_vma=False)
```

```python
import functools

import jax
import jax.numpy as jnp
from jax import lax
from jax.experimental import pallas as pl
from jax.experimental.pallas import tpu as pltpu
from jax.sharding import PartitionSpec as P

MESH = pl.DeviceIdType.MESH
BF = jnp.bfloat16
F32 = jnp.float32
NT = (((1,), (1,)), ((), ()))
NN = (((1,), (0,)), ((), ()))
TN = (((0,), (0,)), ((), ()))


def iota(shape, dim):
    return lax.broadcasted_iota(jnp.int32, shape, dim)


def dot(a, b, dims):
    return lax.dot_general(a, b, dims, preferred_element_type=F32)


def pack(left, right):
    lane = iota((96, 128), 1)
    tail = right[96:128]
    moved = jnp.concatenate([pltpu.roll(tail, 96, 1), pltpu.roll(tail, 64, 1), pltpu.roll(tail, 32, 1)], axis=0)
    return jnp.concatenate([left, jnp.where(lane < 96, right[0:96], moved)], axis=0)


def unpack(packed):
    lane = iota((96, 128), 1)
    low = iota((32, 128), 1)
    rest = packed[128:224]
    top = jnp.where(lane < 96, rest, 0.0)
    tail = jnp.where(
        low < 32,
        pltpu.roll(rest[0:32], 32, 1),
        jnp.where(
            low < 64,
            pltpu.roll(rest[32:64], 64, 1),
            jnp.where(low < 96, pltpu.roll(rest[64:96], 96, 1), 0.0),
        ),
    )
    return packed[0:128], jnp.concatenate([top, tail], axis=0)


def shift_left(a, b, count):
    lane = iota(a.shape, 1)
    return jnp.where(lane < 128 - count, pltpu.roll(a, 128 - count, 1), pltpu.roll(b, 128 - count, 1))


def kernel(
    n_dp,
    ids_ref, prob_ref, tok_ref, cot_ref, wg_ref, wu_ref, wd_ref,
    tg_ref, pg_ref, gg_ref, ug_ref, dg_ref,
    sbuf, rbuf, zbuf, wbuf, wpad, tpad, full, gusend, gurecv, bsend, brecv, scal, delt,
    pbx, pbz, pxr, pzr, rs1s, rs1r, rs2s, rs2r, rets, retr, gradb, tokb, cotb, ssem, rsem, lsem,
):
    exp = lax.axis_index("exp")
    me = lax.axis_index("dp")
    x, z = exp // 4, exp % 4
    xs = [(x + k) % 4 for k in range(4)]
    zs = [(z + k) % 4 for k in range(4)]

    def x_dev(k):
        return {"exp": xs[k] * 4 + z, "dp": me}

    def z_dev(k):
        return {"exp": x * 4 + zs[k], "dp": me}

    counter = [0]

    def remote(src, dst, dev):
        i = counter[0]
        counter[0] += 1
        return pltpu.make_async_remote_copy(
            src_ref=src, dst_ref=dst, send_sem=ssem.at[i], recv_sem=rsem.at[i],
            device_id=dev, device_id_type=MESH,
        )

    pending = []

    def start(copy):
        copy.start()
        pending.append(copy)
        return copy

    barrier = pltpu.get_barrier_semaphore()

    def greet(k, carry):
        pl.semaphore_signal(barrier, inc=1, device_id={"exp": exp, "dp": (me + k) % n_dp}, device_id_type=MESH)
        return carry

    lax.fori_loop(1, n_dp, greet, 0)
    for k in range(1, 4):
        pl.semaphore_signal(barrier, inc=1, device_id=x_dev(k), device_id_type=MESH)
        pl.semaphore_signal(barrier, inc=1, device_id=z_dev(k), device_id_type=MESH)

    own_rows = []
    for n, (ref, held) in enumerate(((tok_ref, tokb), (cot_ref, cotb))):
        copy = pltpu.make_async_copy(ref, held, lsem.at[3 + n])
        copy.start()
        own_rows.append(copy)
    own_w = []
    for a, ref in enumerate((wg_ref, wu_ref, wd_ref)):
        copy = pltpu.make_async_copy(
            ref.at[:, pl.ds(pl.multiple_of(x * 896, 128), 896)], wbuf.at[a, x], lsem.at[a]
        )
        copy.start()
        own_w.append(copy)

    ids = ids_ref[...]
    hot = (iota((n_dp, 128), 0) == ids).astype(F32)
    before = (iota((128, 128), 0) < iota((128, 128), 1)).astype(BF)
    earlier = dot(hot.astype(BF), before, NN)
    slot = jnp.sum(hot * earlier, axis=0, keepdims=True)
    position = ids.astype(F32) * 4.0 + slot

    rows = iota((16 * n_dp, 128), 0)
    row_slot = ((rows >> 4) * 4 + (rows & 3)).astype(F32)
    row_part = (rows >> 2) & 3
    placing = jnp.where(row_slot == position, 1.0, 0.0).astype(BF)
    prob_block = jnp.where(iota((32, 128), 0) == 0, prob_ref[...].astype(F32), 0.0).astype(BF)
    for copy in own_rows:
        copy.wait()
    out = dot(placing, tokb[0:128], NT)
    out = jnp.where(row_part == 1, dot(placing, jnp.concatenate([tokb[128:224], prob_block], axis=0), NT), out)
    out = jnp.where(row_part == 2, dot(placing, cotb[0:128], NT), out)
    zero_block = jnp.zeros((32, 128), BF)
    out = jnp.where(row_part == 3, dot(placing, jnp.concatenate([cotb[128:224], zero_block], axis=0), NT), out)
    sbuf[...] = out.astype(BF).reshape(n_dp, 16, 128)

    pl.semaphore_wait(barrier, n_dp - 1 + 6)

    i_disp = counter[0]
    counter[0] += 1

    def send(k, carry):
        to = (me + k) % n_dp
        pltpu.make_async_remote_copy(
            src_ref=sbuf.at[to], dst_ref=rbuf.at[me], send_sem=ssem.at[i_disp], recv_sem=rsem.at[i_disp],
            device_id={"exp": exp, "dp": to}, device_id_type=MESH,
        ).start()
        return carry

    lax.fori_loop(1, n_dp, send, 0)
    rbuf[me] = sbuf[me]

    w_copies = [
        [
            start(remote(
                ref.at[:, pl.ds(pl.multiple_of(xs[k] * 896, 128), 896)], wbuf.at[a, x], x_dev(k)
            ))
            for k in range(1, 4)
        ]
        for a, ref in enumerate((wg_ref, wu_ref, wd_ref))
    ]

    dispatched = pltpu.make_async_remote_copy(
        src_ref=sbuf.at[pl.ds(0, n_dp - 1)], dst_ref=rbuf.at[pl.ds(0, n_dp - 1)],
        send_sem=ssem.at[i_disp], recv_sem=rsem.at[i_disp], device_id={"exp": exp, "dp": me}, device_id_type=MESH,
    )
    dispatched.wait_recv()

    o, i = iota((256, 256), 0), iota((256, 256), 1)
    order = jnp.where(i == ((o >> 2) & 15) * 16 + (o >> 6) * 4 + (o & 3), 1.0, 0.0).astype(BF)
    groups = []
    for g in range(n_dp // 16):
        groups.append(dot(order, rbuf[16 * g:16 * g + 16].reshape(256, 128), NN))
    parts = [jnp.concatenate([group[64 * j:64 * j + 64] for group in groups], axis=0) for j in range(4)]
    pick = jnp.where((iota((8, 128), 0) == 0) & (iota((8, 128), 1) == 96), 1.0, 0.0).astype(BF)
    weight = dot(pick, parts[1].astype(BF), NT)[0:1]

    def gather_start(h, a):
        mine = zbuf.at[h, a, z]
        halves = [mine.at[pl.ds(0, 112)], mine.at[pl.ds(112, 112)]]
        right = [remote(halves[0], halves[0], z_dev(1)), remote(halves[1], halves[1], z_dev(1))]
        left = [remote(halves[1], halves[1], z_dev(3)), remote(halves[0], halves[0], z_dev(3))]
        for n in range(2):
            start(right[n])
            start(left[n])
        return right, left

    def gather_forward(h, a, right, left):
        from_left = zbuf.at[h, a, zs[3], pl.ds(0, 112)]
        from_right = zbuf.at[h, a, zs[1], pl.ds(112, 112)]
        onward_right = remote(from_left, from_left, z_dev(1))
        onward_left = remote(from_right, from_right, z_dev(3))
        right[0].wait_recv()
        start(onward_right)
        left[0].wait_recv()
        start(onward_left)
        return [right[1], left[1], onward_right, onward_left]

    def gather_rest(copies):
        for copy in copies:
            copy.wait_recv()

    for h in range(2):
        half = slice(128 * h, 128 * h + 128)
        for a in range(2):
            zbuf[h, a, z] = pack(parts[2 * a][half], parts[2 * a + 1][half]).astype(BF)
            if h == 0 and a == 0:
                t0 = gather_start(0, 0)

    def shift_weights(a):
        own_w[a].wait()
        for copy in w_copies[a]:
            copy.wait_recv()
        whole = wbuf[a].reshape(256, 896)
        block = [whole[:, 128 * b:128 * b + 128].astype(F32) for b in range(7)]
        wpad[a, 0] = whole[:, 0:256]
        for n, (first, count) in enumerate(((1, 96), (3, 64), (5, 32))):
            wpad[a, n + 1, :, 0:128] = shift_left(block[first], block[first + 1], count).astype(BF)
            last = block[first + 2] if first + 2 < 7 else block[first + 1]
            wpad[a, n + 1, :, 128:256] = shift_left(block[first + 1], last, count).astype(BF)

    def unpack_all(h, a):
        for n in range(4):
            left, right = unpack(zbuf[h, a, n].astype(F32))
            tpad[a, n, 128 * h:128 * h + 128, 0:128] = left.astype(BF)
            tpad[a, n, 128 * h:128 * h + 128, 128:256] = right.astype(BF)

    def join_all(a):
        part = [[tpad[a, n, :, 128 * h:128 * h + 128].astype(F32) for h in range(2)] for n in range(4)]
        nothing = jnp.zeros((256, 128), F32)
        block = [nothing] * 7
        block[0], block[1] = part[0]
        for n, (first, count) in enumerate(((1, 96), (3, 64), (5, 32))):
            lo, hi = part[n + 1]
            block[first] += shift_left(nothing, lo, 128 - count)
            block[first + 1] += shift_left(lo, hi, 128 - count)
            if first + 2 < 7:
                block[first + 2] += shift_left(hi, nothing, 128 - count)
        for b in range(7):
            full[a, :, 128 * b:128 * b + 128] = block[b].astype(BF)

    def project(h, a, t):
        rows_of = slice(128 * h, 128 * h + 128)
        total = dot(wpad[a, 0], tpad[t, 0, rows_of], NT)
        for n in range(1, 4):
            total += dot(wpad[a, n], tpad[t, n, rows_of], NT)
        return total.reshape(4, 64, 128)

    def to_x(src, dst):
        return [start(remote(src(k), dst(k), x_dev(k))) for k in range(1, 4)]

    def forward_rows(h):
        unpack_all(h, 0)
        gusend[h, :, 0] = project(h, 0, 0)
        gusend[h, :, 1] = project(h, 1, 0)
        return to_x(lambda k: gusend.at[h, xs[k]], lambda k: gurecv.at[h, k - 1])

    def backward_rows(h):
        unpack_all(h, 1)
        bsend[h] = project(h, 2, 1)
        return to_x(lambda k: bsend.at[h, xs[k]], lambda k: brecv.at[h, k - 1])

    def activate(h, copies):
        gather_rest(copies)
        gate = gusend[h, x, 0] + gurecv[h, 0, 0] + gurecv[h, 1, 0] + gurecv[h, 2, 0]
        upper = gusend[h, x, 1] + gurecv[h, 0, 1] + gurecv[h, 1, 1] + gurecv[h, 2, 1]
        sigmoid = jax.nn.sigmoid(gate)
        hidden = gate * sigmoid * upper
        scal[h, x] = (weight[:, 128 * h:128 * h + 128] * hidden).astype(BF)
        sent = to_x(lambda k: scal.at[h, x], lambda k: scal.at[h, x])
        return sent, gate, upper, sigmoid, hidden

    def deltas(h, copies, gate, upper, sigmoid, hidden):
        gather_rest(copies)
        back = bsend[h, x] + brecv[h, 0] + brecv[h, 1] + brecv[h, 2]
        grad = weight[:, 128 * h:128 * h + 128] * back
        delt[h, 0, x] = (grad * upper * sigmoid * (1.0 + gate * (1.0 - sigmoid))).astype(BF)
        delt[h, 1, x] = (grad * gate * sigmoid).astype(BF)
        sent = to_x(lambda k: delt.at[h, :, x], lambda k: delt.at[h, :, x])
        pbx[h] = jnp.broadcast_to(jnp.sum(hidden * back, axis=0, keepdims=True), (8, 128))
        return sent, to_x(lambda k: pbx.at[h], lambda k: pxr.at[h, k - 1])

    def token_part(h, n):
        total = dot(delt[h, 0].reshape(256, 128), wpad[0, n], TN) + dot(delt[h, 1].reshape(256, 128), wpad[1, n], TN)
        return pack(total[:, 0:128], total[:, 128:256])

    def scatter_start(h, copies, prob_copies):
        gather_rest(copies)
        rs1s[h] = token_part(h, zs[2]).astype(BF).reshape(2, 112, 128)
        first = [
            start(remote(rs1s.at[h, 0], rs1r.at[h, 0], z_dev(1))),
            start(remote(rs1s.at[h, 1], rs1r.at[h, 1], z_dev(3))),
        ]
        to_right = token_part(h, zs[1])
        rs2s[h, 0, 1] = to_right[112:224].astype(BF)
        second = [start(remote(rs2s.at[h, 0, 1], rs2r.at[h, 0, 1], z_dev(1)))]
        to_left = token_part(h, zs[3])
        rs2s[h, 1, 0] = to_left[0:112].astype(BF)
        second.append(start(remote(rs2s.at[h, 1, 0], rs2r.at[h, 1, 0], z_dev(3))))
        gather_rest(prob_copies)
        pbz[h] = pbx[h] + pxr[h, 0] + pxr[h, 1] + pxr[h, 2]
        prob = [start(remote(pbz.at[h], pzr.at[h, k - 1], z_dev(k))) for k in range(1, 4)]
        return first, second, prob, to_right, to_left

    def scatter_on(h, first, second, to_right, to_left):
        first[0].wait_recv()
        rs2s[h, 0, 0] = (to_right[0:112] + rs1r[h, 0].astype(F32)).astype(BF)
        second.append(start(remote(rs2s.at[h, 0, 0], rs2r.at[h, 0, 0], z_dev(1))))
        first[1].wait_recv()
        rs2s[h, 1, 1] = (to_left[112:224] + rs1r[h, 1].astype(F32)).astype(BF)
        second.append(start(remote(rs2s.at[h, 1, 1], rs2r.at[h, 1, 1], z_dev(3))))

    i_ret = counter[0]
    counter[0] += 1
    o, i = iota((128, 128), 0), iota((128, 128), 1)
    back_order = jnp.where(i == ((o >> 2) & 1) * 64 + (o >> 3) * 4 + (o & 3), 1.0, 0.0).astype(BF)
    into = jnp.where(
        (iota((8, 128), 0) < 3) & (iota((8, 128), 1) == iota((8, 128), 0) + 96), 1.0, 0.0
    ).astype(BF)

    def finish_rows(h, here, second, prob):
        gather_rest(prob)
        total = (pbz[h] + pzr[h, 0] + pzr[h, 1] + pzr[h, 2])[0:1]
        high = total.astype(BF).astype(F32)
        middle = (total - high).astype(BF).astype(F32)
        low = total - high - middle
        eight = iota((8, 128), 0)
        terms = jnp.where(eight == 0, high, jnp.where(eight == 1, middle, jnp.where(eight == 2, low, 0.0))).astype(BF)
        prob_lanes = dot(terms, into, TN)
        gather_rest(second)
        both = rs2r[h, 0].astype(F32) + rs2r[h, 1].astype(F32)
        left, right = unpack(here + both.reshape(224, 128))
        left = left.astype(BF)
        right = (right + prob_lanes).astype(BF)
        count = n_dp // 2
        for g in range(2):
            piece = jnp.concatenate([left[64 * g:64 * g + 64], right[64 * g:64 * g + 64]], axis=0)
            rets[count * h + 16 * g:count * h + 16 * g + 16] = dot(back_order, piece, NN).reshape(16, 8, 128)

        def send_back(k, carry):
            to = h * count + (me + k) % count

            @pl.when(to != me)
            def _():
                pltpu.make_async_remote_copy(
                    src_ref=rets.at[to], dst_ref=retr.at[me], send_sem=ssem.at[i_ret], recv_sem=rsem.at[i_ret],
                    device_id={"exp": exp, "dp": to}, device_id_type=MESH,
                ).start()

            return carry

        lax.fori_loop(0, count, send_back, 0)

    c0 = gather_start(0, 1)
    shift_weights(0)
    t0_rest = gather_forward(0, 0, *t0)
    t1 = gather_start(1, 0)
    shift_weights(1)
    c0_rest = gather_forward(0, 1, *c0)
    c1 = gather_start(1, 1)
    gather_rest(t0_rest)
    gu0 = forward_rows(0)
    shift_weights(2)
    t1_rest = gather_forward(1, 0, *t1)
    gather_rest(c0_rest)
    b0 = backward_rows(0)
    s0, *kept0 = activate(0, gu0)
    c1_rest = gather_forward(1, 1, *c1)
    d0, p0 = deltas(0, b0, *kept0)
    gather_rest(t1_rest)
    gu1 = forward_rows(1)
    first0, second0, prob0, to_right0, to_left0 = scatter_start(0, d0, p0)
    gather_rest(c1_rest)
    b1 = backward_rows(1)
    s1, *kept1 = activate(1, gu1)
    scatter_on(0, first0, second0, to_right0, to_left0)
    here0 = token_part(0, z)
    d1, p1 = deltas(1, b1, *kept1)
    join_all(0)
    first1, second1, prob1, to_right1, to_left1 = scatter_start(1, d1, p1)
    finish_rows(0, here0, second0, prob0)
    join_all(1)
    scatter_on(1, first1, second1, to_right1, to_left1)
    here1 = token_part(1, z)

    def grad_send(a, lhs, t, ref):
        total = dot(lhs[0].reshape(256, 128), full[t, 0:128], NN) + dot(lhs[1].reshape(256, 128), full[t, 128:256], NN)
        gradb[a] = total.astype(BF).reshape(4, 64, 896)
        lanes = pl.ds(pl.multiple_of(x * 896, 128), 896)
        sent = to_x(lambda k: gradb.at[a, xs[k]], lambda k: ref.at[:, lanes])
        ref[:, lanes] = gradb[a, x]
        return sent

    gather_rest(s0 + s1)
    g_copies = grad_send(2, [scal[0], scal[1]], 1, dg_ref)
    g_copies += grad_send(0, [delt[0, 0], delt[1, 0]], 0, gg_ref)
    g_copies += grad_send(1, [delt[0, 1], delt[1, 1]], 0, ug_ref)
    finish_rows(1, here1, second1, prob1)
    retr[me] = rets[me]
    rows = iota((8 * n_dp, 128), 0)
    match = ((rows >> 3) * 4 + (rows & 3)).astype(F32) == position
    part = (rows >> 2) & 1
    returned = pltpu.make_async_remote_copy(
        src_ref=rets.at[pl.ds(0, n_dp - 1)], dst_ref=retr.at[pl.ds(0, n_dp - 1)],
        send_sem=ssem.at[i_ret], recv_sem=rsem.at[i_ret], device_id={"exp": exp, "dp": me}, device_id_type=MESH,
    )
    returned.wait_recv()
    arrived = retr[...].reshape(8 * n_dp, 128)
    small = arrived.astype(BF)
    tg_ref[0:128] = dot(small, jnp.where(match & (part == 0), 1.0, 0.0).astype(BF), TN).astype(BF)
    tg_ref[128:224] = dot(small, jnp.where(match & (part == 1), 1.0, 0.0).astype(BF), TN)[0:96].astype(BF)
    column = arrived[:, 96:97] + arrived[:, 97:98] + arrived[:, 98:99]
    pg_ref[...] = jnp.sum(jnp.where(match & (part == 1), column, 0.0), axis=0, keepdims=True)

    for copy in g_copies:
        copy.wait_recv()
    dispatched.wait_send()
    returned.wait_send()
    for copy in pending:
        copy.wait_send()


def hand_over(*refs):
    count = len(refs) // 2
    copies = [pltpu.make_async_copy(refs[n], refs[count + n], refs[-1].at[n]) for n in range(count)]
    for copy in copies:
        copy.start()
    for copy in copies:
        copy.wait()


def shards(tokens, cotangent, expert_ids, gate_prob, w_gate, w_up, w_down):
    n_dp = lax.axis_size("dp")
    vmem = pl.BlockSpec(memory_space=pltpu.VMEM)
    hbm = pl.BlockSpec(memory_space=pl.ANY)
    grad = jax.ShapeDtypeStruct((64, 3584), BF)
    made = pl.pallas_call(
        functools.partial(kernel, n_dp),
        out_shape=(
            jax.ShapeDtypeStruct((224, 128), BF),
            jax.ShapeDtypeStruct((1, 128), F32),
            grad, grad, grad,
        ),
        in_specs=[vmem] * 2 + [hbm] * 5,
        out_specs=[vmem] * 5,
        scratch_shapes=[
            pltpu.VMEM((n_dp, 16, 128), BF),
            pltpu.VMEM((n_dp, 16, 128), BF),
            pltpu.VMEM((2, 2, 4, 224, 128), BF),
            pltpu.VMEM((3, 4, 64, 896), BF),
            pltpu.VMEM((3, 4, 256, 256), BF),
            pltpu.VMEM((2, 4, 256, 256), BF),
            pltpu.VMEM((2, 256, 896), BF),
            pltpu.VMEM((2, 4, 2, 64, 128), F32),
            pltpu.VMEM((2, 3, 2, 64, 128), F32),
            pltpu.VMEM((2, 4, 64, 128), F32),
            pltpu.VMEM((2, 3, 64, 128), F32),
            pltpu.VMEM((2, 4, 64, 128), BF),
            pltpu.VMEM((2, 2, 4, 64, 128), BF),
            pltpu.VMEM((2, 8, 128), F32),
            pltpu.VMEM((2, 8, 128), F32),
            pltpu.VMEM((2, 3, 8, 128), F32),
            pltpu.VMEM((2, 3, 8, 128), F32),
            pltpu.VMEM((2, 2, 112, 128), BF),
            pltpu.VMEM((2, 2, 112, 128), BF),
            pltpu.VMEM((2, 2, 2, 112, 128), BF),
            pltpu.VMEM((2, 2, 2, 112, 128), BF),
            pltpu.VMEM((n_dp, 8, 128), F32),
            pltpu.VMEM((n_dp, 8, 128), F32),
            pltpu.VMEM((3, 4, 64, 896), BF),
            pltpu.VMEM((224, 128), BF),
            pltpu.VMEM((224, 128), BF),
            pltpu.SemaphoreType.DMA((96,)),
            pltpu.SemaphoreType.DMA((96,)),
            pltpu.SemaphoreType.DMA((5,)),
        ],
        compiler_params=pltpu.CompilerParams(
            collective_id=0, has_side_effects=True, vmem_limit_bytes=60 * 1024 * 1024
        ),
    )(
        expert_ids.reshape(1, -1), gate_prob.reshape(1, -1), tokens.T, cotangent.T, w_gate[0], w_up[0], w_down[0]
    )
    token_grad, prob_grad, gate_grad, up_grad, down_grad = pl.pallas_call(
        hand_over,
        out_shape=tuple(jax.ShapeDtypeStruct(array.shape, array.dtype) for array in made),
        in_specs=[hbm] * 5,
        out_specs=[hbm] * 5,
        scratch_shapes=[pltpu.SemaphoreType.DMA((5,))],
        compiler_params=pltpu.CompilerParams(vmem_limit_bytes=60 * 1024 * 1024),
    )(*made)
    return token_grad.T, prob_grad.reshape(-1), gate_grad[None], up_grad[None], down_grad[None]


def solution(mesh):
    in_specs = (
        P("dp", "exp"),
        P("dp", "exp"),
        P("dp", None),
        P("dp"),
        P("dp", "exp", None),
        P("dp", "exp", None),
        P("dp", "exp", None),
    )
    out_specs = (
        P("dp", "exp"),
        P("dp"),
        P("dp", "exp", None),
        P("dp", "exp", None),
        P("dp", "exp", None),
    )
    return jax.shard_map(shards, mesh=mesh, in_specs=in_specs, out_specs=out_specs, check_vma=False)
```
